256 devices in a mesh: row: 8 (over y, core), col: 32 (over z, x).
Axes of the slice: x: 4, y: 4, z: 8, core: 2. Of those that a mesh axis runs over, the one named last changes fastest.
Arguments:
- tokens: bfloat16 [2048, 8192], P('row', 'col'), may hold values from -500 to 500
- norm_gain: float32 [8192], replicated, may hold values from 0.1 to 1.9
- gate_weight: bfloat16 [8192, 28672], P('row', 'col'), may hold values from -0.0625 to 0.0625
- up_weight: bfloat16 [8192, 28672], P('row', 'col'), may hold values from -0.0625 to 0.0625
- down_weight: bfloat16 [28672, 8192], P('col', 'row'), may hold values from -0.03125 to 0.03125
Outputs:
- mixed: bfloat16 [2048, 8192], P('col', 'row')
The draws below stay inside these ranges and needn't reach their ends.
All inputs are finite; a program needn't handle non-finite values.
Results may differ from the reference program's by a relative error of at most 0.034.
Values may be sent and summed in bfloat16 or wider, within the bound.
A program may use at most 64 MiB of HBM per device.

```python
import math
import jax
import jax.numpy as jnp
from jax import lax

D = 8192
FF = 28672
TOKENS = 2048
N_ROW = 8


def draw_tokens(key, part):
    key = jax.random.fold_in(key, 11)
    first, second, third = jax.random.split(key, 3)
    base = jnp.clip(jax.random.normal(first, (TOKENS, D), jnp.float32), -6.0, 6.0)
    row_scale = jnp.exp(jax.random.uniform(second, (TOKENS, 1), jnp.float32, 0.0, math.log(10.0)))
    ramp = jnp.exp(math.log(4.0) * jnp.arange(D, dtype=jnp.float32) / D)
    col_scale = ramp * jnp.exp(jax.random.uniform(third, (D,), jnp.float32, -0.69, 0.69))
    return (base * row_scale * col_scale[None, :]).astype(jnp.bfloat16)


def levels(stream_key, shape, pieces, low, largest):
    def one(position, blocks):
        draws = jax.random.uniform(jax.random.fold_in(jax.random.fold_in(stream_key, 6), position), (blocks,), jnp.float32, low / len(pieces), largest / len(pieces))
        return jnp.repeat(jnp.exp(draws), shape[position] // blocks).reshape((-1,) + (1,) * (len(shape) - position - 1))

    gain = one(*pieces[0])
    for cut in pieces[1:]:
        gain = gain * one(*cut)
    return gain


def gaussian(key, shape, deviation, bound, cuts=(), held_as=jnp.bfloat16):
    gain = levels(key, shape, cuts, -0.22, 0.18) if cuts else 1.0
    drawn = jax.random.normal(key, shape, jnp.float32) * deviation * gain
    return jnp.minimum(jnp.maximum(drawn, -bound), bound).astype(held_as)


def setup_inputs(seed: int = 0) -> dict:
    key_of = jax.random.split(jax.random.key(seed), 6)
    tokens = draw_tokens(jax.random.fold_in(key_of[5], 71), 0)
    norm_gain = jnp.clip(1.0 + 0.18 * jax.random.normal(key_of[1], (D,), jnp.float32), 0.1, 1.9)
    gate_weight = gaussian(key_of[2], (D, FF), D ** -0.5, 0.0625, ((0, 8), (1, 32)))
    up_weight = gaussian(key_of[3], (D, FF), D ** -0.5, 0.0625, ((0, 8), (1, 32)))
    down_weight = gaussian(key_of[4], (FF, D), FF ** -0.5, 0.03125, ((0, 32), (1, 8)))
    return {"tokens": tokens, "norm_gain": norm_gain, "gate_weight": gate_weight, "up_weight": up_weight, "down_weight": down_weight}


def reference(tokens, norm_gain, gate_weight, up_weight, down_weight):
    values = tokens.astype(jnp.float32)
    power = lax.optimization_barrier(jnp.mean(values * values, axis=1, keepdims=True))
    normed = (values * lax.rsqrt(power + 1e-05) * norm_gain[None, :]).astype(jnp.bfloat16)
    block = D // N_ROW
    gate = jnp.zeros((TOKENS, FF), jnp.float32)
    up = jnp.zeros((TOKENS, FF), jnp.float32)
    for index in range(N_ROW):
        sliced = normed[:, index * block:(index + 1) * block]
        gate_term = jnp.dot(sliced, gate_weight[index * block:(index + 1) * block], preferred_element_type=jnp.float32).astype(jnp.bfloat16)
        up_term = jnp.dot(sliced, up_weight[index * block:(index + 1) * block], preferred_element_type=jnp.float32).astype(jnp.bfloat16)
        gate_term, up_term = lax.optimization_barrier((gate_term, up_term))
        gate = gate + gate_term.astype(jnp.float32)
        up = up + up_term.astype(jnp.float32)
    hidden = (jax.nn.silu(gate) * up).astype(jnp.bfloat16)
    return jnp.dot(hidden, down_weight, preferred_element_type=jnp.float32).astype(jnp.bfloat16)
```

```python
import functools

import jax
import jax.numpy as jnp
from jax import lax
from jax.experimental import pallas as pl
from jax.experimental.pallas import tpu as pltpu
from jax.sharding import PartitionSpec as P

D = 8192
EPSILON = 1e-05
BF16 = jnp.bfloat16
F32 = jnp.float32

PARTS = 4
S = 64 // PARTS
M = 4 * S
LAG = 4
COPIES = 200


def kernel(
    tok_ref, gain_ref, gate_hbm, up_hbm, down_hbm, out_ref,
    w, wd, st, xs, g, pr, yl, yf, comb, h, o, zl, xl, xd, xf, zb, ss, sx, sz, fb,
    wsem, send_sems, recv_sems,
):
    row = lax.axis_index("row")
    col = lax.axis_index("col")
    y, k = lax.div(row, 2), lax.rem(row, 2)
    z, x = lax.div(col, 4), lax.rem(col, 4)

    def at(ax=0, ay=0, az=0):
        yy = lax.rem(y + ay + 4, 4)
        zz = lax.rem(z + az + 8, 8)
        xx = lax.rem(x + ax + 4, 4)
        return (2 * yy + k, 4 * zz + xx)

    partner = (2 * y + 1 - k, col)
    across = (z, 4 * row + x)
    stays = row == z

    barrier = pltpu.get_barrier_semaphore()

    def greet(device):
        pl.semaphore_signal(barrier, inc=1, device_id=device, device_id_type=pl.DeviceIdType.MESH)

    others = [at(ax=1), at(ax=2), at(ax=3), at(ay=1), at(ay=3), partner]
    others += [at(az=i) for i in range(1, 8)]
    for device in others:
        greet(device)

    loads = [
        pltpu.make_async_copy(gate_hbm, w.at[:, 0:896], wsem.at[0]),
        pltpu.make_async_copy(up_hbm, w.at[:, 896:1792], wsem.at[1]),
        pltpu.make_async_copy(down_hbm, wd, wsem.at[2]),
    ]
    for load in loads:
        load.start()

    @pl.when(jnp.logical_not(stays))
    def _():
        greet(across)

    count = [0]
    started = []

    def make(src, dst, device):
        index = count[0]
        count[0] += 1
        return pltpu.make_async_remote_copy(
            src_ref=src, dst_ref=dst,
            send_sem=send_sems.at[index], recv_sem=recv_sems.at[index],
            device_id=device, device_id_type=pl.DeviceIdType.MESH,
        )

    def send(src, dst, device):
        copy = make(src, dst, device)
        copy.start()
        started.append(copy)
        return copy

    def slot(r):
        r = lax.rem(r + 16, 8)
        return 4 * lax.rem(r, 2) + lax.div(r, 2)

    def piece(xx):
        xx = lax.rem(xx + 8, 4)
        return pl.ds(pl.multiple_of(xx * 256, 256), 256)

    values = tok_ref[...].astype(F32)
    scaled = (values * gain_ref[pl.ds(col, 1), :]).astype(BF16)
    for j in range(PARTS):
        st[j] = scaled[:, j * S:(j + 1) * S, :].reshape(M, 256)
    flat = values.reshape(256, 256)
    squares = jnp.sum(flat * flat, axis=1, keepdims=True)
    diagonal = lax.broadcasted_iota(jnp.int32, (256, 256), 0) == lax.broadcasted_iota(jnp.int32, (256, 256), 1)
    ss[0] = jnp.broadcast_to(jnp.sum(jnp.where(diagonal, squares, 0.0), axis=0, keepdims=True), (8, 256))

    @pl.when(stays)
    def _():
        pl.semaphore_wait(barrier, 13)

    @pl.when(jnp.logical_not(stays))
    def _():
        pl.semaphore_wait(barrier, 14)

    moves = [make(st.at[j], xs.at[j, slot(row), :, piece(x)], across) for j in range(PARTS)]

    @pl.when(jnp.logical_not(stays))
    def _():
        for move in moves:
            move.start()

    @pl.when(stays)
    def _():
        for j in range(PARTS):
            xs[j, slot(row), :, piece(x)] = st[j]

    def arrive(j):
        @pl.when(jnp.logical_not(stays))
        def _():
            moves[j].wait_recv()

    def norm():
        sends = [send(ss.at[0], sx.at[i - 1], at(ax=i)) for i in (1, 2, 3)]
        yield
        yield
        for copy in sends:
            copy.wait_recv()
        ss[1] = ss[0] + sx[0] + sx[1] + sx[2]
        sends = [send(ss.at[1], sz.at[i - 1], at(az=i)) for i in range(1, 8)]
        yield
        yield
        for copy in sends:
            copy.wait_recv()
        total = ss[1]
        for i in range(7):
            total = total + sz[i]
        factor = lax.rsqrt(total[0:1, :] / D + EPSILON)
        column = jnp.sum(jnp.where(diagonal, factor, 0.0), axis=1, keepdims=True)
        fb[...] = jnp.broadcast_to(column, (256, 128)).reshape(4, 64, 128)

    def ring_gather(view, half):
        right = send(view(z), view(z), at(az=1))
        left = send(view(z), view(z), at(az=-1))
        yield
        for step in (1, 2, 3):
            right.wait_recv()
            src = view(z - step) if step < 3 else half(z - step, 0)
            next_right = send(src, src, at(az=1))
            left.wait_recv()
            src = view(z + step) if step < 3 else half(z + step, 1)
            next_left = send(src, src, at(az=-1))
            right, left = next_right, next_left
            yield
        right.wait_recv()
        left.wait_recv()

    def gather_wide_z(j):
        block = xs.at[j, slot(z), :, piece(x)]
        sends = [send(block, block, at(ax=i)) for i in (1, 3, 2)]
        yield
        for copy in sends:
            copy.wait_recv()
        yield from ring_gather(
            lambda zz: xs.at[j, slot(zz)],
            lambda zz, i: xs.at[j, slot(zz), pl.ds(i * (M // 2), M // 2)],
        )

    def gather_wide_x(j):
        yield from ring_gather(
            lambda zz: xs.at[j, slot(zz), :, piece(x)],
            lambda zz, i: xs.at[j, slot(zz), pl.ds(i * (M // 2), M // 2), piece(x)],
        )
        block = xs.at[j, :, :, piece(x)]
        right = send(block, block, at(ax=1))
        left = send(block, block, at(ax=-1))
        yield
        right.wait_recv()
        block = xs.at[j, 0:4, :, piece(x - 1)]
        right = send(block, block, at(ax=1))
        left.wait_recv()
        block = xs.at[j, 4:8, :, piece(x + 1)]
        left = send(block, block, at(ax=-1))
        yield
        right.wait_recv()
        left.wait_recv()

    def gate_up(j, part):
        first = part * 4
        rows = xs.at[j, pl.ds(first, 4)]

        def tile(n, carry):
            cols = pl.ds(pl.multiple_of(n * 256, 256), 256)
            result = jnp.dot(rows[...].reshape(4 * M, 1024), w[:, cols], preferred_element_type=F32)
            g[j, pl.ds(first, 4), :, cols] = result.astype(BF16).reshape(4, M, 256)
            return carry

        lax.fori_loop(0, 7, tile, 0)

    def down(j, part):
        first = part * 4
        rows = h.at[j, pl.ds(first, 4)]

        def tile(n, carry):
            cols = pl.ds(pl.multiple_of(n * 256, 256), 256)
            result = jnp.dot(rows[...].reshape(4 * M, 896), wd[:, cols], preferred_element_type=F32)
            o[j, pl.ds(first, 4), :, :, cols] = result.astype(BF16).reshape(4, 4, S, 256)
            return carry

        lax.fori_loop(0, 4, tile, 0)

    def up32(value):
        return value.astype(F32)

    def ring_reduce(view, landing, width):
        half = width // 2
        lo, hi = pl.ds(0, half), pl.ds(half, half)
        right = send(view(z + 4, lo), landing(0, 0, lo), at(az=1))
        left = send(view(z + 4, hi), landing(1, 0, hi), at(az=-1))
        yield
        full = pl.ds(0, width)
        for step in (1, 2, 3):
            cols = lo if step == 1 else full
            right.wait_recv()
            mine = view(z + 4 - step, cols)
            mine[...] = (up32(mine[...]) + up32(landing(0, step - 1, cols)[...])).astype(BF16)
            mine = view(z + 4 - step, full)
            next_right = send(mine, landing(0, step, full), at(az=1))
            cols = hi if step == 1 else full
            left.wait_recv()
            mine = view(z - 4 + step, cols)
            mine[...] = (up32(mine[...]) + up32(landing(1, step - 1, cols)[...])).astype(BF16)
            mine = view(z - 4 + step, full)
            next_left = send(mine, landing(1, step, full), at(az=-1))
            right, left = next_right, next_left
            yield
        right.wait_recv()
        left.wait_recv()

    def reduce_wide_z(j):
        yield from ring_reduce(
            lambda zz, cols: o.at[j, slot(zz), :, :, cols],
            lambda way, step, cols: zl.at[j, way, step, :, :, cols],
            1024,
        )
        mine = o.at[j, slot(z)]
        mine[...] = (up32(mine[...]) + up32(zl[j, 0, 3]) + up32(zl[j, 1, 3])).astype(BF16)
        sends = [send(mine.at[lax.rem(x + i, 4)], xl.at[j, i - 1], at(ax=i)) for i in (1, 3, 2)]
        yield
        for copy in sends:
            copy.wait_recv()
        total = up32(mine[x]) + up32(xl[j, 0]) + up32(xl[j, 1]) + up32(xl[j, 2])
        out_ref[j * S:(j + 1) * S, :] = total.astype(BF16)

    def reduce_wide_x(j):
        lo, hi = pl.ds(0, 512), pl.ds(512, 512)
        right_x, left_x, far_x = lax.rem(x + 1, 4), lax.rem(x + 3, 4), lax.rem(x + 2, 4)
        right = send(o.at[j, :, far_x, :, lo], xd.at[j, 0], at(ax=1))
        left = send(o.at[j, :, far_x, :, hi], xd.at[j, 1], at(ax=-1))
        plain_right = send(o.at[j, :, right_x, :, hi], xf.at[j, 0], at(ax=1))
        plain_left = send(o.at[j, :, left_x, :, lo], xf.at[j, 1], at(ax=-1))
        yield
        right.wait_recv()
        o[j, :, right_x, :, lo] = (up32(o[j, :, right_x, :, lo]) + up32(xd[j, 0])).astype(BF16)
        right = send(o.at[j, :, right_x, :, lo], xf.at[j, 2], at(ax=1))
        left.wait_recv()
        o[j, :, left_x, :, hi] = (up32(o[j, :, left_x, :, hi]) + up32(xd[j, 1])).astype(BF16)
        left = send(o.at[j, :, left_x, :, hi], xf.at[j, 3], at(ax=-1))
        yield
        plain_right.wait_recv()
        plain_left.wait_recv()
        right.wait_recv()
        left.wait_recv()
        zb[j, 0, :, :, lo] = (up32(o[j, :, x, :, lo]) + up32(xf[j, 1]) + up32(xf[j, 2])).astype(BF16)
        zb[j, 0, :, :, hi] = (up32(o[j, :, x, :, hi]) + up32(xf[j, 0]) + up32(xf[j, 3])).astype(BF16)
        yield from ring_reduce(
            lambda zz, cols: zb.at[j, 0, slot(zz), :, cols],
            lambda way, step, cols: zl.at[j, way, step, 0, :, cols],
            1024,
        )
        total = up32(zb[j, 0, slot(z)]) + up32(zl[j, 0, 3, 0]) + up32(zl[j, 1, 3, 0])
        out_ref[j * S:(j + 1) * S, :] = total.astype(BF16)

    def part(j):
        arrive(j)
        yield from (gather_wide_z if j % 2 == 0 else gather_wide_x)(j)
        if j == 0:
            loads[0].wait()
            loads[1].wait()
        gate_up(j, 1 - k)
        pair = send(g.at[j, pl.ds((1 - k) * 4, 4)], pr.at[j], partner)
        gate_up(j, k)
        yield
        pair.wait_recv()
        ahead, behind, far = lax.rem(y + 1, 4), lax.rem(y + 3, 4), lax.rem(y + 2, 4)

        def add_pair(yy):
            g[j, k * 4 + yy] = (up32(g[j, k * 4 + yy]) + up32(pr[j, yy])).astype(BF16)

        lo, hi = pl.ds(0, 896), pl.ds(896, 896)
        add_pair(far)
        right = send(g.at[j, k * 4 + far, :, lo], yl.at[j, 0], at(ay=1))
        left = send(g.at[j, k * 4 + far, :, hi], yl.at[j, 1], at(ay=-1))
        add_pair(ahead)
        plain_right = send(g.at[j, k * 4 + ahead, :, hi], yf.at[j, 0], at(ay=1))
        add_pair(behind)
        plain_left = send(g.at[j, k * 4 + behind, :, lo], yf.at[j, 1], at(ay=-1))
        add_pair(y)
        yield
        right.wait_recv()
        comb[j, 0] = (up32(g[j, k * 4 + ahead, :, lo]) + up32(yl[j, 0])).astype(BF16)
        right = send(comb.at[j, 0], yf.at[j, 2], at(ay=1))
        left.wait_recv()
        comb[j, 1] = (up32(g[j, k * 4 + behind, :, hi]) + up32(yl[j, 1])).astype(BF16)
        left = send(comb.at[j, 1], yf.at[j, 3], at(ay=-1))
        yield
        plain_right.wait_recv()
        plain_left.wait_recv()
        right.wait_recv()
        left.wait_recv()
        factor = fb[:, j * S:(j + 1) * S, :].reshape(M, 128)[:, 0:1]
        gate = (up32(g[j, k * 4 + y, :, lo]) + up32(yf[j, 1]) + up32(yf[j, 2])) * factor
        up = (up32(g[j, k * 4 + y, :, hi]) + up32(yf[j, 0]) + up32(yf[j, 3])) * factor
        h[j, k * 4 + y] = (gate / (1.0 + jnp.exp(-gate)) * up).astype(BF16)
        block = h.at[j, k * 4 + y]
        right = send(block, block, at(ay=1))
        left = send(block, block, at(ay=-1))
        pairs = [send(block, block, partner)]
        yield
        right.wait_recv()
        src = h.at[j, k * 4 + behind, pl.ds(0, M // 2)]
        next_right = send(src, src, at(ay=1))
        left.wait_recv()
        src = h.at[j, k * 4 + ahead, pl.ds(M // 2, M // 2)]
        next_left = send(src, src, at(ay=-1))
        for yy in (behind, ahead):
            block = h.at[j, k * 4 + yy]
            pairs.append(send(block, block, partner))
        yield
        next_right.wait_recv()
        next_left.wait_recv()
        block = h.at[j, k * 4 + far]
        pairs.append(send(block, block, partner))
        if j == 0:
            loads[2].wait()
        down(j, k)
        for copy in pairs:
            copy.wait_recv()
        down(j, 1 - k)
        yield from (reduce_wide_x if j % 2 == 0 else reduce_wide_z)(j)

    running = [(0, norm())] + [(LAG * j, part(j)) for j in range(PARTS)]
    stage = 0
    while running:
        left_over = []
        for begin, work in running:
            if stage < begin or next(work, "end") != "end":
                left_over.append((begin, work))
        running = left_over
        stage += 1

    @pl.when(jnp.logical_not(stays))
    def _():
        for move in moves:
            move.wait_send()

    for copy in started:
        copy.wait_send()


def local(tokens, norm_gain, gate_weight, up_weight, down_weight):
    vmem = pl.BlockSpec(memory_space=pltpu.VMEM)
    hbm = pl.BlockSpec(memory_space=pl.ANY)
    K = PARTS
    return pl.pallas_call(
        kernel,
        out_shape=jax.ShapeDtypeStruct((64, 1024), BF16),
        in_specs=[vmem, vmem, hbm, hbm, hbm],
        out_specs=vmem,
        scratch_shapes=[
            pltpu.VMEM((1024, 1792), BF16),
            pltpu.VMEM((896, 1024), BF16),
            pltpu.VMEM((K, M, 256), BF16),
            pltpu.VMEM((K, 8, M, 1024), BF16),
            pltpu.VMEM((K, 8, M, 1792), BF16),
            pltpu.VMEM((K, 4, M, 1792), BF16),
            pltpu.VMEM((K, 2, M, 896), BF16),
            pltpu.VMEM((K, 4, M, 896), BF16),
            pltpu.VMEM((K, 2, M, 896), BF16),
            pltpu.VMEM((K, 8, M, 896), BF16),
            pltpu.VMEM((K, 8, 4, S, 1024), BF16),
            pltpu.VMEM((K, 2, 4, 4, S, 1024), BF16),
            pltpu.VMEM((K, 3, S, 1024), BF16),
            pltpu.VMEM((K, 2, 8, S, 512), BF16),
            pltpu.VMEM((K, 4, 8, S, 512), BF16),
            pltpu.VMEM((K, 1, 8, S, 1024), BF16),
            pltpu.VMEM((2, 8, 256), F32),
            pltpu.VMEM((3, 8, 256), F32),
            pltpu.VMEM((7, 8, 256), F32),
            pltpu.VMEM((4, 64, 128), F32),
            pltpu.SemaphoreType.DMA((3,)),
            pltpu.SemaphoreType.DMA((COPIES,)),
            pltpu.SemaphoreType.DMA((COPIES,)),
        ],
        compiler_params=pltpu.CompilerParams(
            collective_id=0, has_side_effects=True, vmem_limit_bytes=58 * 2**20
        ),
        cost_estimate=pl.CostEstimate(flops=11_300_000_000, bytes_accessed=6_000_000, transcendentals=230_000),
        name="swiglu_block",
    )(tokens.reshape(4, 64, 256), norm_gain.reshape(32, 256), gate_weight, up_weight, down_weight)


def solution(mesh):
    return jax.shard_map(
        local,
        mesh=mesh,
        in_specs=(P("row", "col"), P(), P("row", "col"), P("row", "col"), P("col", "row")),
        out_specs=P("col", "row"),
        check_vma=False,
    )
```

```python
import jax
import jax.numpy as jnp
from jax import lax
from jax.experimental import pallas as pl
from jax.experimental.pallas import tpu as pltpu
from jax.sharding import PartitionSpec as P

D = 8192
EPSILON = 1e-05
BF16 = jnp.bfloat16
F32 = jnp.float32
MESH = pl.DeviceIdType.MESH

WAVES = ((0, 1), (1, 2), (3, 2), (5, 2), (7, 1))
START = (0.0, 14.0, 25.0, 37.0, 43.0)
STAGE = (4.0, 4.5, 4.5, 4.5, 4.5)
COPIES = 150


def kernel(
    tok_ref, gain_ref, gate_hbm, up_hbm, down_hbm, out_ref,
    w, wd, st, xs, g, pr, yl, yf, comb, h, o, xd, xf, zb, zl, ss, sx, sz, fa,
    wsem, send_sems, recv_sems,
):
    row = lax.axis_index("row")
    col = lax.axis_index("col")
    y, k = lax.div(row, 2), lax.rem(row, 2)
    z, x = lax.div(col, 4), lax.rem(col, 4)
    ahead, behind, far = lax.rem(y + 1, 4), lax.rem(y + 3, 4), lax.rem(y + 2, 4)
    right_x, left_x, far_x = lax.rem(x + 1, 4), lax.rem(x + 3, 4), lax.rem(x + 2, 4)

    def at(ax=0, ay=0, az=0):
        yy = lax.rem(y + ay + 4, 4)
        zz = lax.rem(z + az + 8, 8)
        xx = lax.rem(x + ax + 4, 4)
        return (2 * yy + k, 4 * zz + xx)

    partner = (2 * y + 1 - k, col)
    rows = [(lax.rem(row + i, 8), col) for i in range(1, 8)]
    perm_target = (z, 4 * lax.rem(row + 4, 8) + x)
    perm_source = (lax.rem(z + 4, 8), 4 * row + x)

    barrier = pltpu.get_barrier_semaphore()
    others = [at(ax=i) for i in (1, 2, 3)] + [at(az=i) for i in range(1, 8)] + rows + [perm_source]
    for device in others:
        pl.semaphore_signal(barrier, inc=1, device_id=device, device_id_type=MESH)

    loads = [
        pltpu.make_async_copy(gate_hbm, w.at[:, 0:896], wsem.at[0]),
        pltpu.make_async_copy(up_hbm, w.at[:, 896:1792], wsem.at[1]),
        pltpu.make_async_copy(down_hbm, wd, wsem.at[2]),
    ]
    for load in loads:
        load.start()

    started = []

    def send(src, dst, device):
        index = len(started)
        copy = pltpu.make_async_remote_copy(
            src_ref=src, dst_ref=dst,
            send_sem=send_sems.at[index], recv_sem=recv_sems.at[index],
            device_id=device, device_id_type=MESH,
        )
        copy.start()
        started.append(copy)
        return copy

    def up32(value):
        return value.astype(F32)

    values = up32(tok_ref[...])
    st[...] = (values * gain_ref[pl.ds(col, 1), :]).astype(BF16)
    squares = jnp.sum(values * values, axis=1, keepdims=True)
    diagonal = lax.broadcasted_iota(jnp.int32, (256, 256), 0) == lax.broadcasted_iota(jnp.int32, (256, 256), 1)
    ss[0] = jnp.broadcast_to(jnp.sum(jnp.where(diagonal, squares, 0.0), axis=0, keepdims=True), (8, 256))

    pl.semaphore_wait(barrier, len(others))

    mine = pl.ds(pl.multiple_of(x * 256, 256), 256)
    move = send(st, xs.at[0, :, mine], perm_target)

    def norm():
        sends = [send(ss.at[0], sx.at[i - 1], at(ax=i)) for i in (1, 2, 3)]
        yield
        for copy in sends:
            copy.wait_recv()
        ss[1] = ss[0] + sx[0] + sx[1] + sx[2]
        sends = [send(ss.at[1], sz.at[i - 1], at(az=i)) for i in range(1, 8)]
        yield
        for copy in sends:
            copy.wait_recv()
        total = ss[1]
        for i in range(7):
            total = total + sz[i]
        fa[row] = lax.rsqrt(total / D + EPSILON)
        sends = [send(fa.at[row], fa.at[row], device) for device in rows]
        yield
        for copy in sends:
            copy.wait_recv()

    arrivals = {}

    def stream():
        move.wait_recv()
        block = xs.at[0, :, mine]
        sends = [send(block, block, at(ax=i)) for i in (1, 3, 2)]
        yield
        for copy in sends:
            copy.wait_recv()
        arrivals[0] = []
        pair = [send(xs.at[0], xs.at[1], at(az=1)), send(xs.at[0], xs.at[2], at(az=-1))]
        for wave in (1, 2, 3):
            yield
            a, b = 2 * wave - 1, 2 * wave
            lo, hi = (pl.ds(0, 128), pl.ds(128, 128)) if wave == 3 else (pl.ds(0, 256), pl.ds(0, 256))
            to_a, to_b = (7, 7) if wave == 3 else (a + 2, b + 2)
            pair[0].wait_recv()
            next_a = send(xs.at[a, lo], xs.at[to_a, lo], at(az=1))
            pair[1].wait_recv()
            next_b = send(xs.at[b, hi], xs.at[to_b, hi], at(az=-1))
            pair = [next_a, next_b]
            arrivals[wave] = []
        arrivals[4] = pair

    def gate_up(blocks, n, half):
        def tile(i, carry):
            cols = pl.ds(pl.multiple_of(i * 256, 256), 256)
            left = xs[blocks, pl.ds(half * 128, 128), :].reshape(n * 128, 1024)
            result = jnp.dot(left, w[:, cols], preferred_element_type=F32)
            g[blocks, half, :, :, cols] = result.astype(BF16).reshape(n, 4, 32, 256)
            return carry

        lax.fori_loop(0, 7, tile, 0)

    def down(blocks, n, half):
        def tile(i, carry):
            cols = pl.ds(pl.multiple_of(i * 256, 256), 256)
            left = h[blocks, half].reshape(n * 128, 896)
            result = jnp.dot(left, wd[:, cols], preferred_element_type=F32)
            o[blocks, pl.ds(half * 2, 2), :, cols] = result.astype(BF16).reshape(n, 2, 64, 256)
            return carry

        lax.fori_loop(0, 4, tile, 0)

    def factors(block):
        if block == 0:
            t = lax.rem(z + 4, 8)
        elif block == 7:
            t = z
        elif block % 2:
            t = lax.rem(z + 12 - (block + 1) // 2, 8)
        else:
            t = lax.rem(z + 4 + block // 2, 8)
        token = lax.broadcasted_iota(jnp.int32, (32, 256), 0) + (k * 128 + y * 32)
        lane = lax.broadcasted_iota(jnp.int32, (32, 256), 1)
        return jnp.sum(jnp.where(token == lane, fa[t, 0:1, :], 0.0), axis=1, keepdims=True)

    chain = {}

    def work(index):
        first, n = WAVES[index]
        blocks = pl.ds(first, n)
        for copy in arrivals[index]:
            copy.wait_recv()
        if index == 0:
            loads[0].wait()
            loads[1].wait()
        gate_up(blocks, n, 1 - k)
        pair = send(g.at[blocks, 1 - k], pr.at[blocks], partner)
        gate_up(blocks, n, k)
        yield
        pair.wait_recv()

        def add_pair(yy):
            g[blocks, k, yy] = (up32(g[blocks, k, yy]) + up32(pr[blocks, yy])).astype(BF16)

        lo, hi = pl.ds(0, 896), pl.ds(896, 896)
        add_pair(far)
        right = send(g.at[blocks, k, far, :, lo], yl.at[0, blocks], at(ay=1))
        left = send(g.at[blocks, k, far, :, hi], yl.at[1, blocks], at(ay=-1))
        add_pair(ahead)
        plain_right = send(g.at[blocks, k, ahead, :, hi], yf.at[0, blocks], at(ay=1))
        add_pair(behind)
        plain_left = send(g.at[blocks, k, behind, :, lo], yf.at[1, blocks], at(ay=-1))
        add_pair(y)
        yield
        right.wait_recv()
        comb[0, blocks] = (up32(g[blocks, k, ahead, :, lo]) + up32(yl[0, blocks])).astype(BF16)
        right = send(comb.at[0, blocks], yf.at[2, blocks], at(ay=1))
        left.wait_recv()
        comb[1, blocks] = (up32(g[blocks, k, behind, :, hi]) + up32(yl[1, blocks])).astype(BF16)
        left = send(comb.at[1, blocks], yf.at[3, blocks], at(ay=-1))
        yield
        for copy in (plain_right, plain_left, right, left):
            copy.wait_recv()
        for block in range(first, first + n):
            factor = factors(block)
            gate = (up32(g[block, k, y, :, lo]) + up32(yf[1, block]) + up32(yf[2, block])) * factor
            up = (up32(g[block, k, y, :, hi]) + up32(yf[0, block]) + up32(yf[3, block])) * factor
            h[block, k, y] = (gate / (1.0 + jnp.exp(-gate)) * up).astype(BF16)
        view = h.at[blocks, k, y]
        right = send(view, view, at(ay=1))
        left = send(view, view, at(ay=-1))
        pairs = [send(view, view, partner)]
        yield
        right.wait_recv()
        view = h.at[blocks, k, behind, pl.ds(0, 16)]
        next_right = send(view, view, at(ay=1))
        left.wait_recv()
        view = h.at[blocks, k, ahead, pl.ds(16, 16)]
        next_left = send(view, view, at(ay=-1))
        for yy in (behind, ahead):
            view = h.at[blocks, k, yy]
            pairs.append(send(view, view, partner))
        yield
        next_right.wait_recv()
        next_left.wait_recv()
        view = h.at[blocks, k, far]
        pairs.append(send(view, view, partner))
        if index == 0:
            loads[2].wait()
        down(blocks, n, k)
        yield
        for copy in pairs:
            copy.wait_recv()
        down(blocks, n, 1 - k)
        lo, hi = pl.ds(0, 512), pl.ds(512, 512)
        right = send(o.at[blocks, far_x, :, lo], xd.at[0, blocks], at(ax=1))
        left = send(o.at[blocks, far_x, :, hi], xd.at[1, blocks], at(ax=-1))
        plain_right = send(o.at[blocks, right_x, :, hi], xf.at[0, blocks], at(ax=1))
        plain_left = send(o.at[blocks, left_x, :, lo], xf.at[1, blocks], at(ax=-1))
        yield
        right.wait_recv()
        o[blocks, right_x, :, lo] = (up32(o[blocks, right_x, :, lo]) + up32(xd[0, blocks])).astype(BF16)
        right = send(o.at[blocks, right_x, :, lo], xf.at[2, blocks], at(ax=1))
        left.wait_recv()
        o[blocks, left_x, :, hi] = (up32(o[blocks, left_x, :, hi]) + up32(xd[1, blocks])).astype(BF16)
        left = send(o.at[blocks, left_x, :, hi], xf.at[3, blocks], at(ax=-1))
        yield
        for copy in (plain_right, plain_left, right, left):
            copy.wait_recv()
        for block in range(first, first + n):
            low = up32(o[block, x, :, lo]) + up32(xf[1, block]) + up32(xf[2, block])
            high = up32(o[block, x, :, hi]) + up32(xf[0, block]) + up32(xf[3, block])
            if index in (1, 2, 3):
                way = (block + 1) % 2
                chain[way].wait_recv()
                if index > 1 or way == 0:
                    low = low + up32(zl[way, index - 1, :, lo])
                if index > 1 or way == 1:
                    high = high + up32(zl[way, index - 1, :, hi])
            if index == 4:
                for way in (0, 1):
                    chain[way].wait_recv()
                    low = low + up32(zl[way, 3, :, lo])
                    high = high + up32(zl[way, 3, :, hi])
                out_ref[:, lo] = low.astype(BF16)
                out_ref[:, hi] = high.astype(BF16)
                continue
            zb[block, :, lo] = low.astype(BF16)
            zb[block, :, hi] = high.astype(BF16)
            if index == 0:
                chain[0] = send(zb.at[0, :, lo], zl.at[0, 0, :, lo], at(az=1))
                chain[1] = send(zb.at[0, :, hi], zl.at[1, 0, :, hi], at(az=-1))
            else:
                chain[way] = send(zb.at[block], zl.at[way, index], at(az=1 if way == 0 else -1))

    steps = []
    for i, when in enumerate((-9.0, -0.5, START[1] - 0.5, START[2] - 0.5, START[3] - 0.5)):
        steps.append((when, 0, "stream"))
    for i, when in enumerate((-10.0, -5.0, 2.0, START[0] + 2.5 * STAGE[0])):
        steps.append((when, 1, "norm"))
    for index in range(5):
        for stage in range(9):
            steps.append((START[index] + stage * STAGE[index], 2 + index, index))
    running = {"stream": stream(), "norm": norm()}
    running.update({index: work(index) for index in range(5)})
    for _, _, name in sorted(steps, key=lambda s: (s[0], s[1])):
        next(running[name], None)

    for copy in started:
        copy.wait_send()


def local(tokens, norm_gain, gate_weight, up_weight, down_weight):
    vmem = pl.BlockSpec(memory_space=pltpu.VMEM)
    hbm = pl.BlockSpec(memory_space=pl.ANY)
    return pl.pallas_call(
        kernel,
        out_shape=jax.ShapeDtypeStruct((64, 1024), BF16),
        in_specs=[vmem, vmem, hbm, hbm, hbm],
        out_specs=vmem,
        scratch_shapes=[
            pltpu.VMEM((1024, 1792), BF16),
            pltpu.VMEM((896, 1024), BF16),
            pltpu.VMEM((256, 256), BF16),
            pltpu.VMEM((8, 256, 1024), BF16),
            pltpu.VMEM((8, 2, 4, 32, 1792), BF16),
            pltpu.VMEM((8, 4, 32, 1792), BF16),
            pltpu.VMEM((2, 8, 32, 896), BF16),
            pltpu.VMEM((4, 8, 32, 896), BF16),
            pltpu.VMEM((2, 8, 32, 896), BF16),
            pltpu.VMEM((8, 2, 4, 32, 896), BF16),
            pltpu.VMEM((8, 4, 64, 1024), BF16),
            pltpu.VMEM((2, 8, 64, 512), BF16),
            pltpu.VMEM((4, 8, 64, 512), BF16),
            pltpu.VMEM((8, 64, 1024), BF16),
            pltpu.VMEM((2, 4, 64, 1024), BF16),
            pltpu.VMEM((2, 8, 256), F32),
            pltpu.VMEM((3, 8, 256), F32),
            pltpu.VMEM((7, 8, 256), F32),
            pltpu.VMEM((8, 8, 256), F32),
            pltpu.SemaphoreType.DMA((3,)),
            pltpu.SemaphoreType.DMA((COPIES,)),
            pltpu.SemaphoreType.DMA((COPIES,)),
        ],
        compiler_params=pltpu.CompilerParams(
            collective_id=0, has_side_effects=True, vmem_limit_bytes=58 * 2**20
        ),
        cost_estimate=pl.CostEstimate(flops=11_300_000_000, bytes_accessed=6_000_000, transcendentals=230_000),
        name="swiglu_block",
    )(tokens, norm_gain.reshape(32, 256), gate_weight, up_weight, down_weight)


def solution(mesh):
    return jax.shard_map(
        local,
        mesh=mesh,
        in_specs=(P("row", "col"), P(), P("row", "col"), P("row", "col"), P("col", "row")),
        out_specs=P("col", "row"),
        check_vma=False,
    )
```

```python
import jax
import jax.numpy as jnp
from jax import lax
from jax.experimental import pallas as pl
from jax.experimental.pallas import tpu as pltpu
from jax.sharding import PartitionSpec as P

D = 8192
EPSILON = 1e-05
BF16 = jnp.bfloat16
F32 = jnp.float32
MESH = pl.DeviceIdType.MESH

GROUPS = (
    (0, 0, 1),
    (1, 1, 1),
    (1, 2, 1),
    (2, 3, 1),
    (2, 4, 1),
    (3, 5, 1),
    (3, 6, 1),
    (4, 7, 1),
)

ORDER = (
    9, 8, 9, 8, 0, 9, 0, 9, 8, 1, 0, 2, 9, 1, 2, 9, 8, 0, 9, 1, 2, 3, 4, 0,
    3, 8, 1, 9, 0, 2, 3, 4, 9, 0, 1, 5, 2, 9, 3, 4, 0, 5, 6, 1, 2, 3, 0, 1,
    2, 4, 7, 5, 6, 3, 1, 4, 3, 5, 2, 6, 7, 4, 1, 5, 4, 6, 3, 7, 2, 5, 4, 6,
    5, 7, 3, 6, 4, 6, 5, 7, 7, 6, 7, 5, 6, 7, 7,
)
COPIES = 260
POOL = 48
WIDE = 96


def kernel(
    tok_ref, gain_ref, gate_hbm, up_hbm, down_hbm, out_ref,
    w, wd, st, xs, g, pr, yl, yf, comb, h, o, xd, xf, zb, zl, ss, sx, sy, fa,
    wsem, send_sems, recv_sems,
):
    row = lax.axis_index("row")
    col = lax.axis_index("col")
    y, k = lax.div(row, 2), lax.rem(row, 2)
    z, x = lax.div(col, 4), lax.rem(col, 4)
    ahead, behind, far = lax.rem(y + 1, 4), lax.rem(y + 3, 4), lax.rem(y + 2, 4)
    right_x, left_x, far_x = lax.rem(x + 1, 4), lax.rem(x + 3, 4), lax.rem(x + 2, 4)

    def at(ax=0, ay=0, az=0):
        yy = lax.rem(y + ay + 4, 4)
        zz = lax.rem(z + az + 8, 8)
        xx = lax.rem(x + ax + 4, 4)
        return (2 * yy + k, 4 * zz + xx)

    partner = (2 * y + 1 - k, col)
    perm_target = (z, 4 * lax.rem(row + 4, 8) + x)
    perm_source = (lax.rem(z + 4, 8), 4 * row + x)

    barrier = pltpu.get_barrier_semaphore()
    others = [perm_source, at(az=1), at(az=-1), at(ax=1), at(ax=2), at(ax=3), at(ay=1), at(ay=-1), partner]
    for device in others:
        pl.semaphore_signal(barrier, inc=1, device_id=device, device_id_type=MESH)

    loads = [
        pltpu.make_async_copy(gate_hbm, w.at[:, 0:896], wsem.at[0]),
        pltpu.make_async_copy(up_hbm, w.at[:, 896:1792], wsem.at[1]),
        pltpu.make_async_copy(down_hbm, wd, wsem.at[2]),
    ]
    for load in loads:
        load.start()

    started = []

    def send(src, dst, device):
        index = len(started)
        if index >= POOL:
            started[index - POOL].wait_send()
        copy = pltpu.make_async_remote_copy(
            src_ref=src, dst_ref=dst,
            send_sem=send_sems.at[index % POOL], recv_sem=recv_sems.at[index],
            device_id=device, device_id_type=MESH,
        )
        copy.start()
        started.append(copy)
        return copy

    def up32(value):
        return value.astype(F32)

    values = up32(tok_ref[...])
    st[...] = (values * gain_ref[pl.ds(pl.multiple_of(col * 256, 256), 256)].reshape(1, 256)).astype(BF16)
    squares = jnp.sum(values * values, axis=1, keepdims=True)
    diagonal = lax.broadcasted_iota(jnp.int32, (256, 256), 0) == lax.broadcasted_iota(jnp.int32, (256, 256), 1)
    ss[0] = jnp.broadcast_to(jnp.sum(jnp.where(diagonal, squares, 0.0), axis=0, keepdims=True), (8, 256))

    pl.semaphore_wait(barrier, len(others))

    mine = pl.ds(pl.multiple_of(x * 256, 256), 256)
    moves = [
        send(st.at[part], xs.at[0, part, mine], perm_target)
        for part in (pl.ds(0, WIDE), pl.ds(WIDE, 256 - WIDE)) if part.size
    ]

    square_move = send(ss.at[0], ss.at[1], perm_target)

    def norm():
        yield
        square_move.wait_recv()
        sends = [send(ss.at[1], sx.at[i - 1], at(ax=i)) for i in (1, 2, 3)]
        yield
        for copy in sends:
            copy.wait_recv()
        ss[2] = ss[1] + sx[0] + sx[1] + sx[2]
        copy = send(ss.at[2], sy.at[3], partner)
        yield
        copy.wait_recv()
        ss[3] = ss[2] + sy[3]
        right, left = send(ss.at[3], sy.at[0], at(ay=1)), send(ss.at[3], sy.at[1], at(ay=-1))
        yield
        right.wait_recv()
        right = send(sy.at[0], sy.at[2], at(ay=1))
        left.wait_recv()
        yield
        right.wait_recv()
        fa[0] = lax.rsqrt((ss[3] + sy[0] + sy[1] + sy[2]) / D + EPSILON)
        right, left = send(fa.at[0], fa.at[1], at(az=1)), send(fa.at[0], fa.at[2], at(az=-1))
        for wave in (1, 2):
            yield
            right.wait_recv()
            right = send(fa.at[2 * wave - 1], fa.at[2 * wave + 1], at(az=1))
            left.wait_recv()
            left = send(fa.at[2 * wave], fa.at[2 * wave + 2], at(az=-1))
        yield
        right.wait_recv()
        right = send(fa.at[5], fa.at[7], at(az=1))
        left.wait_recv()
        yield
        right.wait_recv()

    arrivals = {}

    def stream():
        wide, narrow = pl.ds(0, WIDE), pl.ds(WIDE, 256 - WIDE)

        def over_x(blocks, part):
            view = xs.at[blocks, part, mine]
            return [send(view, view, at(ax=i)) for i in (1, 3, 2)]

        def halves(first, size):
            return pl.ds(first, size // 2), pl.ds(first + size // 2, size // 2)

        def forward(wave, part, cols):
            if wave == 0:
                source, target, rows_of = (0, 0), (1, 2), (part, part)
            elif wave < 3:
                source, target, rows_of = (2 * wave - 1, 2 * wave), (2 * wave + 1, 2 * wave + 2), (part, part)
            else:
                source, target, rows_of = (5, 6), (7, 7), halves(part.start, part.size)
            copies = []
            for way in (0, 1):
                if wave > 0:
                    ring[part.start][way].wait_recv()
                copies.append(send(
                    xs.at[source[way], rows_of[way], cols], xs.at[target[way], rows_of[way], cols],
                    at(az=1 - 2 * way)))
            ring[part.start] = copies

        everything = pl.ds(0, 1024)
        ring = {}
        for move in moves:
            move.wait_recv()
            if move is moves[0]:
                gathered = over_x(0, wide)
        if WIDE < 256:
            forward(0, narrow, mine)
            arrivals[0] = over_x(0, narrow)
        yield
        for copy in gathered:
            copy.wait_recv()
        forward(0, wide, everything)
        for wave in (1, 2, 3, 4):
            if WIDE < 256:
                if wave < 4:
                    forward(wave, narrow, mine)
                else:
                    for copy in ring[WIDE]:
                        copy.wait_recv()
                for group, (arrival, first, n) in enumerate(GROUPS):
                    if arrival == wave:
                        arrivals[group] = over_x(pl.ds(first, n), narrow)
            if wave < 4:
                yield
                forward(wave, wide, everything)
        arrivals[len(GROUPS) - 1] = arrivals.get(len(GROUPS) - 1, []) + ring[0]

    def gate_up(blocks, n, half, count):
        def tile(i, carry):
            cols = pl.ds(pl.multiple_of(i * 256, 256), 256)
            left = xs[blocks, pl.ds(half * 128, count * 128), :].reshape(n * count * 128, 1024)
            result = jnp.dot(left, w[:, cols], preferred_element_type=F32)
            g[blocks, pl.ds(half, count), :, :, cols] = result.astype(BF16).reshape(n, count, 4, 32, 256)
            return carry

        lax.fori_loop(0, 7, tile, 0, unroll=True)

    def down(blocks, n, half):
        def tile(i, carry):
            cols = pl.ds(pl.multiple_of(i * 256, 256), 256)
            left = h[blocks, half].reshape(n * 128, 896)
            result = jnp.dot(left, wd[:, cols], preferred_element_type=F32)
            o[blocks, pl.ds(half * 2, 2), :, cols] = result.astype(BF16).reshape(n, 2, 64, 256)
            return carry

        lax.fori_loop(0, 4, tile, 0, unroll=True)

    def factors(block):
        token = lax.broadcasted_iota(jnp.int32, (32, 256), 0) + (k * 128 + y * 32)
        lane = lax.broadcasted_iota(jnp.int32, (32, 256), 1)
        return jnp.sum(jnp.where(token == lane, fa[block, 0:1, :], 0.0), axis=1, keepdims=True)

    chain = {}

    def work(index):
        wave, first, n = GROUPS[index]
        blocks = pl.ds(first, n)
        for copy in arrivals.get(index, []):
            copy.wait_recv()
        if index == 0:
            loads[0].wait()
            loads[1].wait()
        gate_up(blocks, n, 1 - k, 1)
        pair = send(g.at[blocks, 1 - k], pr.at[blocks], partner)
        gate_up(blocks, n, k, 1)
        yield
        pair.wait_recv()

        def add_pair(yy):
            g[blocks, k, yy] = (up32(g[blocks, k, yy]) + up32(pr[blocks, yy])).astype(BF16)

        lo, hi = pl.ds(0, 896), pl.ds(896, 896)
        add_pair(far)
        right = send(g.at[blocks, k, far, :, lo], yl.at[0, blocks], at(ay=1))
        left = send(g.at[blocks, k, far, :, hi], yl.at[1, blocks], at(ay=-1))
        add_pair(ahead)
        plain_right = send(g.at[blocks, k, ahead, :, hi], yf.at[0, blocks], at(ay=1))
        add_pair(behind)
        plain_left = send(g.at[blocks, k, behind, :, lo], yf.at[1, blocks], at(ay=-1))
        add_pair(y)
        yield
        right.wait_recv()
        comb[0, blocks] = (up32(g[blocks, k, ahead, :, lo]) + up32(yl[0, blocks])).astype(BF16)
        right = send(comb.at[0, blocks], yf.at[2, blocks], at(ay=1))
        left.wait_recv()
        comb[1, blocks] = (up32(g[blocks, k, behind, :, hi]) + up32(yl[1, blocks])).astype(BF16)
        left = send(comb.at[1, blocks], yf.at[3, blocks], at(ay=-1))
        yield
        sums = [plain_right, plain_left, right, left]
        for copy in sums:
            copy.wait_recv()
        for block in range(first, first + n):
            factor = factors(block)
            gate, up = up32(g[block, k, y, :, lo]), up32(g[block, k, y, :, hi])
            gate = (gate + up32(yf[1, block]) + up32(yf[2, block])) * factor
            up = (up + up32(yf[0, block]) + up32(yf[3, block])) * factor
            h[block, k, y] = (gate / (1.0 + jnp.exp(-gate)) * up).astype(BF16)
        view = h.at[blocks, k, y]
        pairs = []

        def to_partner(*places):
            for yy in places:
                view = h.at[blocks, k, yy]
                pairs.append(send(view, view, partner))

        right = send(view, view, at(ay=1))
        left = send(view, view, at(ay=-1))
        to_partner(y)
        yield
        right.wait_recv()
        view = h.at[blocks, k, behind, pl.ds(0, 16)]
        next_right = send(view, view, at(ay=1))
        left.wait_recv()
        view = h.at[blocks, k, ahead, pl.ds(16, 16)]
        next_left = send(view, view, at(ay=-1))
        to_partner(behind, ahead)
        yield
        next_right.wait_recv()
        next_left.wait_recv()
        to_partner(far)
        if index == 0:
            loads[2].wait()
        down(blocks, n, k)
        yield
        for copy in pairs:
            copy.wait_recv()
        down(blocks, n, 1 - k)
        lo, hi = pl.ds(0, 512), pl.ds(512, 512)
        right = send(o.at[blocks, far_x, :, lo], xd.at[0, blocks], at(ax=1))
        left = send(o.at[blocks, far_x, :, hi], xd.at[1, blocks], at(ax=-1))
        plain_right = send(o.at[blocks, right_x, :, hi], xf.at[0, blocks], at(ax=1))
        plain_left = send(o.at[blocks, left_x, :, lo], xf.at[1, blocks], at(ax=-1))
        yield
        right.wait_recv()
        o[blocks, right_x, :, lo] = (up32(o[blocks, right_x, :, lo]) + up32(xd[0, blocks])).astype(BF16)
        right = send(o.at[blocks, right_x, :, lo], xf.at[2, blocks], at(ax=1))
        left.wait_recv()
        o[blocks, left_x, :, hi] = (up32(o[blocks, left_x, :, hi]) + up32(xd[1, blocks])).astype(BF16)
        left = send(o.at[blocks, left_x, :, hi], xf.at[3, blocks], at(ax=-1))
        yield
        sums = [plain_right, plain_left, right, left]
        for copy in sums:
            copy.wait_recv()
        for block in range(first, first + n):
            low, high = up32(o[block, x, :, lo]), up32(o[block, x, :, hi])
            low = low + up32(xf[1, block]) + up32(xf[2, block])
            high = high + up32(xf[0, block]) + up32(xf[3, block])
            if wave in (1, 2, 3):
                way = (block + 1) % 2
                chain[way].wait_recv()
                if wave > 1 or way == 0:
                    low = low + up32(zl[way, wave - 1, :, lo])
                if wave > 1 or way == 1:
                    high = high + up32(zl[way, wave - 1, :, hi])
            if wave == 4:
                for way in (0, 1):
                    chain[way].wait_recv()
                    low = low + up32(zl[way, 3, :, lo])
                    high = high + up32(zl[way, 3, :, hi])
                out_ref[:, lo] = low.astype(BF16)
                out_ref[:, hi] = high.astype(BF16)
                continue
            zb[block, :, lo] = low.astype(BF16)
            zb[block, :, hi] = high.astype(BF16)
            if wave == 0:
                chain[0] = send(zb.at[0, :, lo], zl.at[0, 0, :, lo], at(az=1))
                chain[1] = send(zb.at[0, :, hi], zl.at[1, 0, :, hi], at(az=-1))
            else:
                chain[way] = send(zb.at[block], zl.at[way, wave], at(az=1 if way == 0 else -1))

    running = [work(index) for index in range(len(GROUPS))] + [stream(), norm()]
    for name in ORDER:
        next(running[name], None)

    for copy in started[-POOL:]:
        copy.wait_send()


def local(tokens, norm_gain, gate_weight, up_weight, down_weight):
    vmem = pl.BlockSpec(memory_space=pltpu.VMEM)
    hbm = pl.BlockSpec(memory_space=pl.ANY)
    return pl.pallas_call(
        kernel,
        out_shape=jax.ShapeDtypeStruct((64, 1024), BF16),
        in_specs=[vmem, vmem, hbm, hbm, hbm],
        out_specs=vmem,
        scratch_shapes=[
            pltpu.VMEM((1024, 1792), BF16),
            pltpu.VMEM((896, 1024), BF16),
            pltpu.VMEM((256, 256), BF16),
            pltpu.VMEM((8, 256, 1024), BF16),
            pltpu.VMEM((8, 2, 4, 32, 1792), BF16),
            pltpu.VMEM((8, 4, 32, 1792), BF16),
            pltpu.VMEM((2, 8, 32, 896), BF16),
            pltpu.VMEM((4, 8, 32, 896), BF16),
            pltpu.VMEM((2, 8, 32, 896), BF16),
            pltpu.VMEM((8, 2, 4, 32, 896), BF16),
            pltpu.VMEM((8, 4, 64, 1024), BF16),
            pltpu.VMEM((2, 8, 64, 512), BF16),
            pltpu.VMEM((4, 8, 64, 512), BF16),
            pltpu.VMEM((8, 64, 1024), BF16),
            pltpu.VMEM((2, 4, 64, 1024), BF16),
            pltpu.VMEM((4, 8, 256), F32),
            pltpu.VMEM((3, 8, 256), F32),
            pltpu.VMEM((4, 8, 256), F32),
            pltpu.VMEM((8, 8, 256), F32),
            pltpu.SemaphoreType.DMA((3,)),
            pltpu.SemaphoreType.DMA((POOL,)),
            pltpu.SemaphoreType.DMA((COPIES,)),
        ],
        compiler_params=pltpu.CompilerParams(
            collective_id=0, has_side_effects=True, vmem_limit_bytes=58 * 2**20
        ),
        cost_estimate=pl.CostEstimate(flops=11_300_000_000, bytes_accessed=6_000_000, transcendentals=230_000),
        name="swiglu_block",
    )(tokens, norm_gain, gate_weight, up_weight, down_weight)


def solution(mesh):
    return jax.shard_map(
        local,
        mesh=mesh,
        in_specs=(P("row", "col"), P(), P("row", "col"), P("row", "col"), P("col", "row")),
        out_specs=P("col", "row"),
        check_vma=False,
    )
```

```python
import jax
import jax.numpy as jnp
from jax import lax
from jax.experimental import pallas as pl
from jax.experimental.pallas import tpu as pltpu
from jax.sharding import PartitionSpec as P

D = 8192
EPSILON = 1e-05
BF16 = jnp.bfloat16
F32 = jnp.float32
MESH = pl.DeviceIdType.MESH

GROUPS = (
    (0, 0, 1),
    (1, 1, 1),
    (1, 2, 1),
    (2, 3, 1),
    (2, 4, 1),
    (3, 5, 1),
    (3, 6, 1),
    (4, 7, 1),
)

ORDER = (
    9, 8, 9, 8, 0, 9, 0, 9, 8, 1, 0, 2, 9, 1, 2, 9, 8, 0, 9, 1, 2, 3, 4, 0,
    3, 8, 1, 9, 0, 2, 3, 4, 9, 0, 1, 5, 2, 9, 3, 4, 0, 5, 6, 1, 2, 3, 0, 1,
    2, 4, 7, 5, 6, 3, 1, 4, 3, 5, 2, 6, 7, 4, 1, 5, 4, 6, 3, 7, 2, 5, 4, 6,
    5, 7, 3, 6, 4, 6, 5, 7, 7, 6, 7, 5, 6, 7, 7,
)
COPIES = 140
POOL = 24
WIDE = 96


def kernel(
    tok_ref, gain_ref, gate_hbm, up_hbm, down_hbm, out_ref,
    w, wd, st, xs, g, pr, yl, yf, comb, h, o, xd, xf, zb, zl, ss, sx, sy, fa,
    wsem, send_sems, recv_sems,
):
    row = lax.axis_index("row")
    col = lax.axis_index("col")
    y, k = lax.div(row, 2), lax.rem(row, 2)
    z, x = lax.div(col, 4), lax.rem(col, 4)
    ahead, behind, far = lax.rem(y + 1, 4), lax.rem(y + 3, 4), lax.rem(y + 2, 4)
    right_x, left_x, far_x = lax.rem(x + 1, 4), lax.rem(x + 3, 4), lax.rem(x + 2, 4)

    def at(ax=0, ay=0, az=0):
        yy = lax.rem(y + ay + 4, 4)
        zz = lax.rem(z + az + 8, 8)
        xx = lax.rem(x + ax + 4, 4)
        return (2 * yy + k, 4 * zz + xx)

    partner = (2 * y + 1 - k, col)
    perm_target = (z, 4 * lax.rem(row + 4, 8) + x)
    perm_source = (lax.rem(z + 4, 8), 4 * row + x)

    barrier = pltpu.get_barrier_semaphore()
    others = [perm_source, at(az=1), at(az=-1), at(ax=1), at(ax=2), at(ax=3), at(ay=1), at(ay=-1), partner]
    for device in others:
        pl.semaphore_signal(barrier, inc=1, device_id=device, device_id_type=MESH)

    loads = [
        pltpu.make_async_copy(gate_hbm, w.at[:, 0:896], wsem.at[0]),
        pltpu.make_async_copy(up_hbm, w.at[:, 896:1792], wsem.at[1]),
        pltpu.make_async_copy(down_hbm, wd, wsem.at[2]),
    ]
    for load in loads:
        load.start()

    started = []
    used = [0]

    def arrival():
        used[0] += 1
        return recv_sems.at[used[0] - 1]

    def wait_for(sem, view):
        pltpu.make_async_copy(view, view, sem).wait()

    def send(src, dst, device, sem=None):
        index = len(started)
        if index >= POOL:
            started[index - POOL].wait_send()
        copy = pltpu.make_async_remote_copy(
            src_ref=src, dst_ref=dst,
            send_sem=send_sems.at[index % POOL], recv_sem=arrival() if sem is None else sem,
            device_id=device, device_id_type=MESH,
        )
        copy.start()
        started.append(copy)
        return copy

    def up32(value):
        return value.astype(F32)

    values = up32(tok_ref[...])
    st[...] = (values * gain_ref[pl.ds(pl.multiple_of(col * 256, 256), 256)].reshape(1, 256)).astype(BF16)
    squares = jnp.sum(values * values, axis=1, keepdims=True)
    diagonal = lax.broadcasted_iota(jnp.int32, (256, 256), 0) == lax.broadcasted_iota(jnp.int32, (256, 256), 1)
    ss[0] = jnp.broadcast_to(jnp.sum(jnp.where(diagonal, squares, 0.0), axis=0, keepdims=True), (8, 256))

    pl.semaphore_wait(barrier, len(others))

    mine = pl.ds(pl.multiple_of(x * 256, 256), 256)
    moves = [
        send(st.at[part], xs.at[0, part, mine], perm_target)
        for part in (pl.ds(0, WIDE), pl.ds(WIDE, 256 - WIDE)) if part.size
    ]

    square_move = send(ss.at[0], ss.at[1], perm_target)

    def norm():
        yield
        square_move.wait_recv()
        sem = arrival()
        for i in (1, 2, 3):
            send(ss.at[1], sx.at[i - 1], at(ax=i), sem)
        yield
        wait_for(sem, sx)
        ss[2] = ss[1] + sx[0] + sx[1] + sx[2]
        copy = send(ss.at[2], sy.at[3], partner)
        yield
        copy.wait_recv()
        ss[3] = ss[2] + sy[3]
        right, left = send(ss.at[3], sy.at[0], at(ay=1)), send(ss.at[3], sy.at[1], at(ay=-1))
        yield
        right.wait_recv()
        right = send(sy.at[0], sy.at[2], at(ay=1))
        left.wait_recv()
        yield
        right.wait_recv()
        fa[0] = lax.rsqrt((ss[3] + sy[0] + sy[1] + sy[2]) / D + EPSILON)
        right, left = send(fa.at[0], fa.at[1], at(az=1)), send(fa.at[0], fa.at[2], at(az=-1))
        for wave in (1, 2):
            yield
            right.wait_recv()
            right = send(fa.at[2 * wave - 1], fa.at[2 * wave + 1], at(az=1))
            left.wait_recv()
            left = send(fa.at[2 * wave], fa.at[2 * wave + 2], at(az=-1))
        yield
        right.wait_recv()
        right = send(fa.at[5], fa.at[7], at(az=1))
        left.wait_recv()
        yield
        right.wait_recv()

    arrivals = {}

    def stream():
        wide, narrow = pl.ds(0, WIDE), pl.ds(WIDE, 256 - WIDE)

        def over_x(blocks, part):
            view, sem = xs.at[blocks, part, mine], arrival()
            for i in (1, 3, 2):
                send(view, view, at(ax=i), sem)
            return lambda: wait_for(sem, xs.at[blocks, part, 0:768])

        def halves(first, size):
            return pl.ds(first, size // 2), pl.ds(first + size // 2, size // 2)

        def forward(wave, part, cols):
            if wave == 0:
                source, target, rows_of = (0, 0), (1, 2), (part, part)
            elif wave < 3:
                source, target, rows_of = (2 * wave - 1, 2 * wave), (2 * wave + 1, 2 * wave + 2), (part, part)
            else:
                source, target, rows_of = (5, 6), (7, 7), halves(part.start, part.size)
            copies = []
            for way in (0, 1):
                if wave > 0:
                    ring[part.start][way].wait_recv()
                copies.append(send(
                    xs.at[source[way], rows_of[way], cols], xs.at[target[way], rows_of[way], cols],
                    at(az=1 - 2 * way)))
            ring[part.start] = copies

        everything = pl.ds(0, 1024)
        ring = {}
        for move in moves:
            move.wait_recv()
            if move is moves[0]:
                gathered = over_x(0, wide)
        forward(0, narrow, mine)
        arrivals[0] = over_x(0, narrow)
        yield
        gathered()
        forward(0, wide, everything)
        for wave in (1, 2, 3, 4):
            if wave < 4:
                forward(wave, narrow, mine)
            else:
                for copy in ring[WIDE]:
                    copy.wait_recv()
            for group, (arrives, first, n) in enumerate(GROUPS):
                if arrives == wave:
                    arrivals[group] = over_x(pl.ds(first, n), narrow)
            if wave < 4:
                yield
                forward(wave, wide, everything)
        arrivals["last"] = ring[0]

    def gate_up(blocks, n, half, count):
        def tile(i, carry):
            cols = pl.ds(pl.multiple_of(i * 256, 256), 256)
            left = xs[blocks, pl.ds(half * 128, count * 128), :].reshape(n * count * 128, 1024)
            result = jnp.dot(left, w[:, cols], preferred_element_type=F32)
            g[blocks, pl.ds(half, count), :, :, cols] = result.astype(BF16).reshape(n, count, 4, 32, 256)
            return carry

        lax.fori_loop(0, 7, tile, 0, unroll=True)

    def down(blocks, n, half):
        def tile(i, carry):
            cols = pl.ds(pl.multiple_of(i * 256, 256), 256)
            left = h[blocks, half].reshape(n * 128, 896)
            result = jnp.dot(left, wd[:, cols], preferred_element_type=F32)
            o[blocks, pl.ds(half * 2, 2), :, cols] = result.astype(BF16).reshape(n, 2, 64, 256)
            return carry

        lax.fori_loop(0, 4, tile, 0, unroll=True)

    def factors(block):
        token = lax.broadcasted_iota(jnp.int32, (32, 256), 0) + (k * 128 + y * 32)
        lane = lax.broadcasted_iota(jnp.int32, (32, 256), 1)
        return jnp.sum(jnp.where(token == lane, fa[block, 0:1, :], 0.0), axis=1, keepdims=True)

    chain = {}

    def work(index):
        wave, first, n = GROUPS[index]
        blocks = pl.ds(first, n)
        arrivals[index]()
        if wave == 4:
            for copy in arrivals["last"]:
                copy.wait_recv()
        if index == 0:
            loads[0].wait()
            loads[1].wait()
        gate_up(blocks, n, 1 - k, 1)
        pair = send(g.at[blocks, 1 - k], pr.at[blocks], partner)
        gate_up(blocks, n, k, 1)
        yield
        pair.wait_recv()

        def add_pair(yy):
            g[blocks, k, yy] = (up32(g[blocks, k, yy]) + up32(pr[blocks, yy])).astype(BF16)

        lo, hi = pl.ds(0, 896), pl.ds(896, 896)
        add_pair(far)
        right = send(g.at[blocks, k, far, :, lo], yl.at[0, blocks], at(ay=1))
        left = send(g.at[blocks, k, far, :, hi], yl.at[1, blocks], at(ay=-1))
        add_pair(ahead)
        final = arrival()
        send(g.at[blocks, k, ahead, :, hi], yf.at[0, blocks], at(ay=1), final)
        add_pair(behind)
        send(g.at[blocks, k, behind, :, lo], yf.at[1, blocks], at(ay=-1), final)
        add_pair(y)
        yield
        right.wait_recv()
        comb[0, blocks] = (up32(g[blocks, k, ahead, :, lo]) + up32(yl[0, blocks])).astype(BF16)
        send(comb.at[0, blocks], yf.at[2, blocks], at(ay=1), final)
        left.wait_recv()
        comb[1, blocks] = (up32(g[blocks, k, behind, :, hi]) + up32(yl[1, blocks])).astype(BF16)
        send(comb.at[1, blocks], yf.at[3, blocks], at(ay=-1), final)
        yield
        wait_for(final, yf.at[:, blocks])
        for block in range(first, first + n):
            factor = factors(block)
            gate, up = up32(g[block, k, y, :, lo]), up32(g[block, k, y, :, hi])
            gate = (gate + up32(yf[1, block]) + up32(yf[2, block])) * factor
            up = (up + up32(yf[0, block]) + up32(yf[3, block])) * factor
            h[block, k, y] = (gate / (1.0 + jnp.exp(-gate)) * up).astype(BF16)
        view = h.at[blocks, k, y]
        pairs, across = arrival(), arrival()

        def to_partner(*places):
            for yy in places:
                view = h.at[blocks, k, yy]
                send(view, view, partner, pairs)

        right = send(view, view, at(ay=1))
        left = send(view, view, at(ay=-1))
        to_partner(y)
        yield
        right.wait_recv()
        view = h.at[blocks, k, behind, pl.ds(0, 16)]
        send(view, view, at(ay=1), across)
        left.wait_recv()
        view = h.at[blocks, k, ahead, pl.ds(16, 16)]
        send(view, view, at(ay=-1), across)
        to_partner(behind, ahead)
        yield
        wait_for(across, h.at[blocks, k, far])
        to_partner(far)
        if index == 0:
            loads[2].wait()
        down(blocks, n, k)
        yield
        wait_for(pairs, h.at[blocks, 1 - k])
        down(blocks, n, 1 - k)
        lo, hi = pl.ds(0, 512), pl.ds(512, 512)
        right = send(o.at[blocks, far_x, :, lo], xd.at[0, blocks], at(ax=1))
        left = send(o.at[blocks, far_x, :, hi], xd.at[1, blocks], at(ax=-1))
        final = arrival()
        send(o.at[blocks, right_x, :, hi], xf.at[0, blocks], at(ax=1), final)
        send(o.at[blocks, left_x, :, lo], xf.at[1, blocks], at(ax=-1), final)
        yield
        right.wait_recv()
        o[blocks, right_x, :, lo] = (up32(o[blocks, right_x, :, lo]) + up32(xd[0, blocks])).astype(BF16)
        send(o.at[blocks, right_x, :, lo], xf.at[2, blocks], at(ax=1), final)
        left.wait_recv()
        o[blocks, left_x, :, hi] = (up32(o[blocks, left_x, :, hi]) + up32(xd[1, blocks])).astype(BF16)
        send(o.at[blocks, left_x, :, hi], xf.at[3, blocks], at(ax=-1), final)
        yield
        wait_for(final, xf.at[:, blocks])
        for block in range(first, first + n):
            low, high = up32(o[block, x, :, lo]), up32(o[block, x, :, hi])
            low = low + up32(xf[1, block]) + up32(xf[2, block])
            high = high + up32(xf[0, block]) + up32(xf[3, block])
            if wave in (1, 2, 3):
                way = (block + 1) % 2
                chain[way].wait_recv()
                if wave > 1 or way == 0:
                    low = low + up32(zl[way, wave - 1, :, lo])
                if wave > 1 or way == 1:
                    high = high + up32(zl[way, wave - 1, :, hi])
            if wave == 4:
                for way in (0, 1):
                    chain[way].wait_recv()
                    low = low + up32(zl[way, 3, :, lo])
                    high = high + up32(zl[way, 3, :, hi])
                out_ref[:, lo] = low.astype(BF16)
                out_ref[:, hi] = high.astype(BF16)
                continue
            zb[block, :, lo] = low.astype(BF16)
            zb[block, :, hi] = high.astype(BF16)
            if wave == 0:
                chain[0] = send(zb.at[0, :, lo], zl.at[0, 0, :, lo], at(az=1))
                chain[1] = send(zb.at[0, :, hi], zl.at[1, 0, :, hi], at(az=-1))
            else:
                chain[way] = send(zb.at[block], zl.at[way, wave], at(az=1 if way == 0 else -1))

    running = [work(index) for index in range(len(GROUPS))] + [stream(), norm()]
    for name in ORDER:
        next(running[name], None)

    assert used[0] <= COPIES
    for copy in started[-POOL:]:
        copy.wait_send()


def local(tokens, norm_gain, gate_weight, up_weight, down_weight):
    vmem = pl.BlockSpec(memory_space=pltpu.VMEM)
    hbm = pl.BlockSpec(memory_space=pl.ANY)
    return pl.pallas_call(
        kernel,
        out_shape=jax.ShapeDtypeStruct((64, 1024), BF16),
        in_specs=[vmem, vmem, hbm, hbm, hbm],
        out_specs=vmem,
        scratch_shapes=[
            pltpu.VMEM((1024, 1792), BF16),
            pltpu.VMEM((896, 1024), BF16),
            pltpu.VMEM((256, 256), BF16),
            pltpu.VMEM((8, 256, 1024), BF16),
            pltpu.VMEM((8, 2, 4, 32, 1792), BF16),
            pltpu.VMEM((8, 4, 32, 1792), BF16),
            pltpu.VMEM((2, 8, 32, 896), BF16),
            pltpu.VMEM((4, 8, 32, 896), BF16),
            pltpu.VMEM((2, 8, 32, 896), BF16),
            pltpu.VMEM((8, 2, 4, 32, 896), BF16),
            pltpu.VMEM((8, 4, 64, 1024), BF16),
            pltpu.VMEM((2, 8, 64, 512), BF16),
            pltpu.VMEM((4, 8, 64, 512), BF16),
            pltpu.VMEM((8, 64, 1024), BF16),
            pltpu.VMEM((2, 4, 64, 1024), BF16),
            pltpu.VMEM((4, 8, 256), F32),
            pltpu.VMEM((3, 8, 256), F32),
            pltpu.VMEM((4, 8, 256), F32),
            pltpu.VMEM((8, 8, 256), F32),
            pltpu.SemaphoreType.DMA((3,)),
            pltpu.SemaphoreType.DMA((POOL,)),
            pltpu.SemaphoreType.DMA((COPIES,)),
        ],
        compiler_params=pltpu.CompilerParams(
            collective_id=0, has_side_effects=True, vmem_limit_bytes=58 * 2**20
        ),
        cost_estimate=pl.CostEstimate(flops=11_300_000_000, bytes_accessed=6_000_000, transcendentals=230_000),
        name="swiglu_block",
    )(tokens, norm_gain, gate_weight, up_weight, down_weight)


def solution(mesh):
    return jax.shard_map(
        local,
        mesh=mesh,
        in_specs=(P("row", "col"), P(), P("row", "col"), P("row", "col"), P("col", "row")),
        out_specs=P("col", "row"),
        check_vma=False,
    )
```
